32 devices in a mesh: seq: 8 (over y, x, core), head: 4 (over z).
Axes of the slice: x: 2, y: 2, z: 4, core: 2. Of those that a mesh axis runs over, the one named last changes fastest.
Arguments:
- queries: bfloat16 [2048, 768], P('seq', 'head'), may hold values from -9 to 9
- keys: bfloat16 [2048, 768], P('seq', 'head'), may hold values from -12 to 12
- values: bfloat16 [2048, 768], P('seq', 'head'), may hold values from -6 to 6
- out_weight: bfloat16 [768, 1536], replicated, may hold values from -0.21875 to 0.21875
- out_grad: bfloat16 [2048, 1536], P('seq', 'head'), may hold values from -6 to 6
Outputs:
- projected: bfloat16 [2048, 1536], P('seq', 'head')
- query_grad: bfloat16 [2048, 768], P('seq', 'head')
- key_grad: bfloat16 [2048, 768], P('seq', 'head')
- value_grad: bfloat16 [2048, 768], P('seq', 'head')
The draws below stay inside these ranges and needn't reach their ends.
All inputs are finite; a program needn't handle non-finite values.
Results may differ from the reference program's by a relative error of at most 0.02.
Values may be sent and summed in bfloat16 or wider, within the bound.
A program may use at most 128 MiB of HBM per device.

```python
import math
import jax
import jax.numpy as jnp
from jax import lax

D = 1536
HEADS = 12
HD = 64
NC = 2048


def draw_queries(key, part):
    base = jnp.clip(1.5 * jax.random.normal(jax.random.fold_in(key, 1), (NC, HEADS * HD), jnp.float32), -9.0, 9.0)
    return base.astype(jnp.bfloat16)


def draw_keys(key, part):
    base = jnp.clip(2.0 * jax.random.normal(jax.random.fold_in(key, 2), (NC, HEADS * HD), jnp.float32), -12.0, 12.0)
    return base.astype(jnp.bfloat16)


def level_of(rng, extent, pieces, least, high):
    def one(axis_at, blocks):
        steps = jax.random.uniform(jax.random.fold_in(jax.random.fold_in(rng, 6), axis_at), (blocks,), jnp.float32, least / len(pieces), high / len(pieces))
        return jnp.repeat(jnp.exp(steps), extent[axis_at] // blocks).reshape((-1,) + (1,) * (len(extent) - axis_at - 1))

    loudness = one(*pieces[0])
    for cut in pieces[1:]:
        loudness = loudness * one(*cut)
    return loudness


def gaussian(key, extent, deviation, bound, pieces=(), kind=jnp.bfloat16):
    entries = deviation * jax.random.normal(key, extent, jnp.float32)
    if pieces:
        entries = entries * level_of(key, extent, pieces, -0.22, 0.18)
    return jnp.clip(entries, -bound, bound).astype(kind)


def setup_inputs(seed: int = 0) -> dict:
    splits = jax.random.split(jax.random.key(seed), 6)
    queries = draw_queries(jax.random.fold_in(splits[5], 71), 0)
    keys = draw_keys(jax.random.fold_in(splits[5], 71), 0)
    values = gaussian(splits[2], (NC, HEADS * HD), 1.0, 6.0, ((0, 8), (1, 4)))
    out_weight = gaussian(splits[3], (HEADS * HD, D), (HEADS * HD) ** -0.5, 0.21875)
    out_grad = gaussian(splits[4], (NC, D), 1.0, 6.0, ((0, 8), (1, 4)))
    return dict(queries=queries, keys=keys, values=values, out_weight=out_weight, out_grad=out_grad)


masked_score = -1e30


def head_forward(query_head, key_head, value_head):
    count_rows = query_head.shape[0]
    block_rows = math.gcd(512, count_rows)
    key_pos = jnp.arange(count_rows, dtype=jnp.int32)
    score_scale = HD ** -0.5

    def query_block(block_index):
        first_row = block_index * block_rows
        query_part = lax.dynamic_slice_in_dim(query_head, first_row, block_rows, 0)
        scores = jnp.dot(query_part, key_head.T, preferred_element_type=jnp.float32) * score_scale
        query_pos = first_row + jnp.arange(block_rows, dtype=jnp.int32)
        causal = key_pos[None, :] <= query_pos[:, None]
        scores = jnp.where(causal, scores, masked_score)
        row_max = jnp.max(scores, axis=1, keepdims=True)
        weights = jnp.where(causal, jnp.exp(scores - row_max), 0.0)
        denominator = jnp.sum(weights, axis=1, keepdims=True)
        mixed = jnp.dot(weights.astype(jnp.bfloat16), value_head, preferred_element_type=jnp.float32) / denominator
        return mixed.astype(jnp.bfloat16), (row_max + jnp.log(denominator))[:, 0]

    outputs, log_total = lax.map(query_block, jnp.arange(count_rows // block_rows, dtype=jnp.int32))
    return outputs.reshape(count_rows, HD), log_total.reshape(count_rows)


def head_backward(query_head, key_head, value_head, grad_head, log_total, row_dot):
    count_rows = query_head.shape[0]
    block_rows = math.gcd(512, count_rows)
    all_pos = jnp.arange(count_rows, dtype=jnp.int32)
    score_scale = HD ** -0.5

    def query_block(block_index):
        first_row = block_index * block_rows
        query_part = lax.dynamic_slice_in_dim(query_head, first_row, block_rows, 0)
        grad_part = lax.dynamic_slice_in_dim(grad_head, first_row, block_rows, 0)
        log_part = lax.dynamic_slice_in_dim(log_total, first_row, block_rows, 0)
        dot_part = lax.dynamic_slice_in_dim(row_dot, first_row, block_rows, 0)
        query_pos = first_row + jnp.arange(block_rows, dtype=jnp.int32)
        causal = all_pos[None, :] <= query_pos[:, None]
        scores = jnp.dot(query_part, key_head.T, preferred_element_type=jnp.float32) * score_scale
        scores = jnp.where(causal, scores, masked_score)
        probability = jnp.exp(scores - log_part[:, None])
        prob_grad = jnp.dot(grad_part, value_head.T, preferred_element_type=jnp.float32)
        dscore = probability * (prob_grad - dot_part[:, None])
        result = jnp.dot(dscore.astype(jnp.bfloat16), key_head, preferred_element_type=jnp.float32) * score_scale
        return result.astype(jnp.bfloat16)

    def key_block(block_index):
        first_row = block_index * block_rows
        key_part = lax.dynamic_slice_in_dim(key_head, first_row, block_rows, 0)
        value_part = lax.dynamic_slice_in_dim(value_head, first_row, block_rows, 0)
        key_pos = first_row + jnp.arange(block_rows, dtype=jnp.int32)
        causal = key_pos[None, :] <= all_pos[:, None]
        scores = jnp.dot(query_head, key_part.T, preferred_element_type=jnp.float32) * score_scale
        scores = jnp.where(causal, scores, masked_score)
        probability = jnp.exp(scores - log_total[:, None])
        value_result = jnp.dot(probability.astype(jnp.bfloat16).T, grad_head, preferred_element_type=jnp.float32)
        prob_grad = jnp.dot(grad_head, value_part.T, preferred_element_type=jnp.float32)
        dscore = probability * (prob_grad - row_dot[:, None])
        key_result = jnp.dot(dscore.astype(jnp.bfloat16).T, query_head, preferred_element_type=jnp.float32) * score_scale
        return key_result.astype(jnp.bfloat16), value_result.astype(jnp.bfloat16)

    block_ids = jnp.arange(count_rows // block_rows, dtype=jnp.int32)
    query_result = lax.map(query_block, block_ids).reshape(count_rows, HD)
    key_result, value_result = lax.map(key_block, block_ids)
    return query_result, key_result.reshape(count_rows, HD), value_result.reshape(count_rows, HD)


def reference(queries, keys, values, out_weight, out_grad):
    count_rows = queries.shape[0]

    def by_head(matrix):
        return matrix.reshape(count_rows, HEADS, HD).transpose(1, 0, 2)

    def merge_heads(stacked):
        return stacked.transpose(1, 0, 2).reshape(count_rows, HEADS * HD)

    def forward_one(triple):
        return head_forward(triple[0], triple[1], triple[2])

    query_heads, key_heads, value_heads = by_head(queries), by_head(keys), by_head(values)
    attended_heads, log_total = lax.map(forward_one, (query_heads, key_heads, value_heads))
    attended = merge_heads(attended_heads)
    projected = jnp.dot(attended, out_weight, preferred_element_type=jnp.float32).astype(jnp.bfloat16)
    output_grad = lax.dot_general(out_grad, out_weight, (((1,), (1,)), ((), ())), preferred_element_type=jnp.float32).astype(jnp.bfloat16)
    row_dot = jnp.sum((output_grad.astype(jnp.float32) * attended.astype(jnp.float32)).reshape(count_rows, HEADS, HD), axis=2).T

    def backward_one(group_args):
        return head_backward(group_args[0], group_args[1], group_args[2], group_args[3], group_args[4], group_args[5])

    query_result, key_result, value_result = lax.map(backward_one, (query_heads, key_heads, value_heads, by_head(output_grad), log_total, row_dot))
    return projected, merge_heads(query_result), merge_heads(key_result), merge_heads(value_result)
```

```python
import functools
import math

import jax
import jax.numpy as jnp
from jax import lax
from jax.experimental import pallas as pl
from jax.experimental.pallas import tpu as pltpu
from jax.sharding import PartitionSpec as P

HD = 64
MESH = pl.DeviceIdType.MESH
masked_score = -1e30


def round_up(value, unit):
    return -(-value // unit) * unit


def nt(left, right):
    return lax.dot_general(
        left, right, (((1,), (1,)), ((), ())), preferred_element_type=jnp.float32
    )


def nn(left, right):
    return jnp.dot(left, right, preferred_element_type=jnp.float32)


def kernel(
    n, m, q_ref, k_ref, v_ref, w_ref, og_ref,
    proj_ref, qg_ref, kg_ref, vg_ref,
    kv, qd, lr, part, got, att, wpad, qm, dom, km, vm,
    acc_a, acc_b, acc_c, max_s, sum_s, dot_s,
    w_sem, kv_send, kv_recv, qd_send, qd_recv, lr_send, lr_recv,
    pg_send, pg_recv, at_send, at_recv,
):
    rows, width = q_ref.shape
    cols = og_ref.shape[1]
    heads = width // HD
    wide = round_up(width, 128)
    pad = wide - width
    low = slice(0, wide)
    high = slice(2 * width - wide, 2 * width)
    half = rows // 2
    stat_rows = lr.shape[1]
    scale = HD ** (-0.5)
    factor = scale / math.log(2.0)
    me = lax.axis_index("seq")
    hz = lax.axis_index("head")

    def w_copy(j):
        return pltpu.make_async_copy(
            w_ref.at[pl.ds(j * width, width), pl.ds(pl.multiple_of(hz * cols, 128), cols)],
            wpad.at[j, pl.ds(pad, width), :],
            w_sem.at[j],
        )

    for j in range(m):
        w_copy(j).start()

    barrier = pltpu.get_barrier_semaphore()
    for step in range(1, m):
        other = lax.rem(hz + step, m)
        pl.semaphore_signal(barrier, inc=1, device_id=(me, other), device_id_type=MESH)

    def greet(step, carry):
        other = lax.rem(me + step, n)
        pl.semaphore_signal(barrier, inc=1, device_id=(other, hz), device_id_type=MESH)
        return carry

    lax.fori_loop(1, n, greet, 0)

    kv[me] = jnp.concatenate([k_ref[...], v_ref[...]], axis=1)
    pl.semaphore_wait(barrier, n - 1 + m - 1)

    def seq_copy(buf, send, recv, slot, dst):
        return pltpu.make_async_remote_copy(
            src_ref=buf.at[slot], dst_ref=buf.at[slot],
            send_sem=send.at[dst], recv_sem=recv.at[slot],
            device_id=(dst, hz), device_id_type=MESH,
        )

    def send_kv(j, carry):
        seq_copy(kv, kv_send, kv_recv, me, j).start()
        return carry

    lax.fori_loop(me + 1, n, send_kv, 0)

    for j in range(m):
        w_copy(j).wait()

    def share(j):
        return nt(wpad[j, pad:pad + width, :], og_ref[...])

    def part_copy(dst):
        return pltpu.make_async_remote_copy(
            src_ref=part.at[dst], dst_ref=got.at[hz],
            send_sem=pg_send.at[dst], recv_sem=pg_recv.at[hz],
            device_id=(me, dst), device_id_type=MESH,
        )

    for step in range(1, m):
        other = lax.rem(hz + step, m)
        part[other] = share(other).astype(jnp.bfloat16)
        part_copy(other).start()
    own_share = share(hz)

    lane = lax.broadcasted_iota(jnp.int32, (rows, wide), 1)

    def low_mask(h):
        return (lane >= h * HD) & (lane < (h + 1) * HD)

    def high_mask(h):
        return (lane >= pad + h * HD) & (lane < pad + (h + 1) * HD)

    q_wide = jnp.concatenate([q_ref[...], jnp.zeros((rows, pad), jnp.bfloat16)], axis=1)
    zero_16 = jnp.zeros((rows, wide), jnp.bfloat16)
    own_k = kv[me][:, low]
    own_v = kv[me][:, high]
    for h in range(heads):
        qm[h] = jnp.where(low_mask(h), q_wide, zero_16)
        km[h] = jnp.where(low_mask(h), own_k, zero_16)
        vm[h] = jnp.where(high_mask(h), own_v, zero_16)

    row_id = lax.broadcasted_iota(jnp.int32, (rows, rows), 0)
    col_id = lax.broadcasted_iota(jnp.int32, (rows, rows), 1)

    for h in range(heads):
        s = nt(qm[h], own_k) * factor
        s = jnp.where(col_id <= row_id, s, masked_score)
        top = jnp.max(s, axis=1, keepdims=True)
        e = jnp.exp2(s - top)
        max_s[h] = top
        sum_s[h] = jnp.sum(e, axis=1, keepdims=True)
        acc_a[h] = nn(e.astype(jnp.bfloat16), own_v)

    total = own_share
    for step in range(1, m):
        other = lax.rem(hz + step, m)
        pltpu.make_async_remote_copy(
            src_ref=part.at[other], dst_ref=got.at[other],
            send_sem=pg_send.at[other], recv_sem=pg_recv.at[other],
            device_id=(me, other), device_id_type=MESH,
        ).wait_recv()
        total = total + got[other].astype(jnp.float32)
    grad = total.T.astype(jnp.bfloat16)
    qd[me] = jnp.concatenate([q_ref[...], grad], axis=1)

    def send_qd(j, carry):
        seq_copy(qd, qd_send, qd_recv, me, me - 1 - j).start()
        return carry

    lax.fori_loop(0, me, send_qd, 0)
    own_g = qd[me][:, high]
    for h in range(heads):
        dom[h] = jnp.where(high_mask(h), own_g, zero_16)

    def forward(i, carry):
        j = me - 1 - i
        seq_copy(kv, kv_send, kv_recv, j, me).wait_recv()
        block = kv.at[j]
        for h in range(heads):
            s = nt(qm[h], block[:, low]) * factor
            old = max_s[h]
            top = jnp.maximum(old, jnp.max(s, axis=1, keepdims=True))
            alpha = jnp.exp2(old - top)
            e = jnp.exp2(s - top)
            max_s[h] = top
            sum_s[h] = sum_s[h] * alpha + jnp.sum(e, axis=1, keepdims=True)
            acc_a[h] = acc_a[h] * alpha + nn(e.astype(jnp.bfloat16), block[:, high])
        return carry

    lax.fori_loop(0, me, forward, 0)

    mixed = jnp.zeros((rows, wide), jnp.float32)
    for h in range(heads):
        mixed = jnp.where(high_mask(h), acc_a[h] * (1.0 / sum_s[h]), mixed)
    attended = mixed.astype(jnp.bfloat16).astype(jnp.float32)
    upper = attended[:half, pad:]
    lower = attended[half:, pad:]
    att[hz] = jnp.concatenate([upper, lower], axis=1).astype(jnp.bfloat16)

    def att_copy(slot, dst):
        return pltpu.make_async_remote_copy(
            src_ref=att.at[slot], dst_ref=att.at[slot],
            send_sem=at_send.at[dst], recv_sem=at_recv.at[slot],
            device_id=(me, dst), device_id_type=MESH,
        )

    for step in range(1, m):
        att_copy(hz, lax.rem(hz + step, m)).start()

    product = attended * own_g.astype(jnp.float32)
    stat_lane = lax.broadcasted_iota(jnp.int32, (rows, 128), 1)
    stats = jnp.zeros((rows, 128), jnp.float32)
    for h in range(heads):
        row_dot = jnp.sum(jnp.where(high_mask(h), product, 0.0), axis=1, keepdims=True)
        log_total = max_s[h] + jnp.log2(sum_s[h])
        max_s[h] = log_total
        dot_s[h] = row_dot
        stats = jnp.where(stat_lane == h, log_total, stats)
        stats = jnp.where(stat_lane == heads + h, row_dot, stats)
    lr[me] = stats.T[:stat_rows, :]

    def send_lr(j, carry):
        seq_copy(lr, lr_send, lr_recv, me, j).start()
        return carry

    lax.fori_loop(0, me, send_lr, 0)

    def query_step(block, h, own):
        s = nt(qm[h], block[:, low]) * factor
        if own:
            s = jnp.where(col_id <= row_id, s, masked_score)
        p = jnp.exp2(s - max_s[h])
        ds = p * (nt(dom[h], block[:, high]) - dot_s[h])
        return nn(ds.astype(jnp.bfloat16), block[:, low])

    for h in range(heads):
        acc_a[h] = query_step(kv.at[me], h, True)

    def query_loop(i, carry):
        block = kv.at[i]
        for h in range(heads):
            acc_a[h] = acc_a[h] + query_step(block, h, False)
        return carry

    lax.fori_loop(0, me, query_loop, 0)
    query_sum = jnp.zeros((rows, wide), jnp.float32)
    for h in range(heads):
        query_sum = jnp.where(low_mask(h), acc_a[h], query_sum)
    qg_ref[...] = (query_sum * scale).astype(jnp.bfloat16)[:, :width]

    def key_step(block, stat, h, own):
        s = nt(km[h], block[:, low]) * factor
        if own:
            s = jnp.where(row_id <= col_id, s, masked_score)
        p = jnp.exp2(s - stat[h:h + 1, :])
        value_part = nn(p.astype(jnp.bfloat16), block[:, high])
        ds = p * (nt(vm[h], block[:, high]) - stat[heads + h:heads + h + 1, :])
        return nn(ds.astype(jnp.bfloat16), block[:, low]), value_part

    for h in range(heads):
        acc_b[h], acc_c[h] = key_step(qd.at[me], lr.at[me], h, True)

    wpad[:, 0:pad, :] = jnp.zeros((m, pad, cols), jnp.bfloat16)
    wpad[:, pad + width:, :] = jnp.zeros((m, pad, cols), jnp.bfloat16)

    def project(slot):
        block = att.at[slot]
        return (
            nn(block[:, low], wpad[slot, pad:, :]),
            nn(block[:, high], wpad[slot, :wide, :]),
        )

    proj_top, proj_low = project(hz)
    for step in range(1, m):
        other = lax.rem(hz + step, m)
        att_copy(other, hz).wait_recv()
        more_top, more_low = project(other)
        proj_top = proj_top + more_top
        proj_low = proj_low + more_low
    proj_ref[:half, :] = proj_top.astype(jnp.bfloat16)
    proj_ref[half:, :] = proj_low.astype(jnp.bfloat16)

    def key_loop(j, carry):
        seq_copy(qd, qd_send, qd_recv, j, me).wait_recv()
        seq_copy(lr, lr_send, lr_recv, j, me).wait_recv()
        for h in range(heads):
            key_part, value_part = key_step(qd.at[j], lr.at[j], h, False)
            acc_b[h] = acc_b[h] + key_part
            acc_c[h] = acc_c[h] + value_part
        return carry

    lax.fori_loop(me + 1, n, key_loop, 0)
    key_sum = jnp.zeros((rows, wide), jnp.float32)
    value_sum = jnp.zeros((rows, wide), jnp.float32)
    for h in range(heads):
        key_sum = jnp.where(low_mask(h), acc_b[h], key_sum)
        value_sum = jnp.where(high_mask(h), acc_c[h], value_sum)
    kg_ref[...] = (key_sum * scale).astype(jnp.bfloat16)[:, :width]
    vg_ref[...] = value_sum[:, pad:].astype(jnp.bfloat16)

    def sent_kv(j, carry):
        seq_copy(kv, kv_send, kv_recv, me, j).wait_send()
        return carry

    lax.fori_loop(me + 1, n, sent_kv, 0)

    def sent_back(j, carry):
        seq_copy(qd, qd_send, qd_recv, me, j).wait_send()
        seq_copy(lr, lr_send, lr_recv, me, j).wait_send()
        return carry

    lax.fori_loop(0, me, sent_back, 0)
    for step in range(1, m):
        other = lax.rem(hz + step, m)
        part_copy(other).wait_send()
        att_copy(hz, other).wait_send()


def per_device(n, m, queries, keys, values, out_weight, out_grad):
    rows, width = queries.shape
    cols = out_grad.shape[1]
    heads = width // HD
    wide = round_up(width, 128)
    pad = wide - width
    stat_rows = round_up(2 * heads, 8)
    bf16, f32 = jnp.bfloat16, jnp.float32
    in_vmem = pl.BlockSpec(memory_space=pltpu.VMEM)
    dma = pltpu.SemaphoreType.DMA
    macs = rows * rows * n * 9 * width + 2 * rows * width * m * cols
    return pl.pallas_call(
        functools.partial(kernel, n, m),
        out_shape=(
            jax.ShapeDtypeStruct((rows, cols), bf16),
            jax.ShapeDtypeStruct((rows, width), bf16),
            jax.ShapeDtypeStruct((rows, width), bf16),
            jax.ShapeDtypeStruct((rows, width), bf16),
        ),
        in_specs=[in_vmem, in_vmem, in_vmem, pl.BlockSpec(memory_space=pl.ANY), in_vmem],
        out_specs=(in_vmem,) * 4,
        scratch_shapes=[
            pltpu.VMEM((n, rows, 2 * width), bf16),
            pltpu.VMEM((n, rows, 2 * width), bf16),
            pltpu.VMEM((n, stat_rows, rows), f32),
            pltpu.VMEM((m, width, rows), bf16),
            pltpu.VMEM((m, width, rows), bf16),
            pltpu.VMEM((m, rows // 2, 2 * width), bf16),
            pltpu.VMEM((m, pad + width + pad, cols), bf16),
        ]
        + [pltpu.VMEM((heads, rows, wide), bf16)] * 4
        + [pltpu.VMEM((heads, rows, wide), f32)] * 3
        + [pltpu.VMEM((heads, rows, 1), f32)] * 3
        + [dma((m,))]
        + [dma((n,))] * 6
        + [dma((m,))] * 4,
        compiler_params=pltpu.CompilerParams(
            collective_id=0, has_side_effects=True, vmem_limit_bytes=56 * 1024 * 1024
        ),
        cost_estimate=pl.CostEstimate(
            flops=macs, bytes_accessed=6 * rows * width * 2, transcendentals=rows * rows * n * heads
        ),
    )(queries, keys, values, out_weight, out_grad)


def solution(mesh):
    return jax.shard_map(
        functools.partial(per_device, mesh.shape["seq"], mesh.shape["head"]),
        mesh=mesh,
        in_specs=(P("seq", "head"), P("seq", "head"), P("seq", "head"), P(), P("seq", "head")),
        out_specs=(P("seq", "head"), P("seq", "head"), P("seq", "head"), P("seq", "head")),
        check_vma=False,
    )
```

```python
import functools
import math

import jax
import jax.numpy as jnp
from jax import lax
from jax.experimental import pallas as pl
from jax.experimental.pallas import tpu as pltpu
from jax.sharding import PartitionSpec as P

HD = 64
MESH = pl.DeviceIdType.MESH
masked_score = -1e30


def round_up(value, unit):
    return -(-value // unit) * unit


def nt(left, right):
    return lax.dot_general(
        left, right, (((1,), (1,)), ((), ())), preferred_element_type=jnp.float32
    )


def nn(left, right):
    return jnp.dot(left, right, preferred_element_type=jnp.float32)


def kernel(
    n, m, q_ref, k_ref, v_ref, w_ref, og_ref,
    proj_ref, qg_ref, kg_ref, vg_ref,
    kv, qd, lr, part, got, att, wpad, qm, dom, km, vm,
    acc_a, acc_b, acc_c, max_s, sum_s, dot_s,
    w_sem, kv_send, kv_recv, qd_send, qd_recv, lr_send, lr_recv,
    pg_send, pg_recv, at_send, at_recv, kv_pass, qd_pass,
):
    width, rows = q_ref.shape
    cols = og_ref.shape[1]
    heads = width // HD
    wide = round_up(width, 128)
    pad = wide - width
    low = slice(0, wide)
    high = slice(2 * width - wide, 2 * width)
    half = rows // 2
    stat_rows = lr.shape[1]
    scale = HD ** (-0.5)
    factor = scale / math.log(2.0)
    me = lax.axis_index("seq")
    hz = lax.axis_index("head")
    parity = lax.rem(me, 2)
    pair = lax.div(me, 2)
    sibling = 2 * pair + 1 - parity

    def w_copy(j):
        return pltpu.make_async_copy(
            w_ref.at[pl.ds(j * width, width), pl.ds(pl.multiple_of(hz * cols, 128), cols)],
            wpad.at[j, pl.ds(pad, width), :],
            w_sem.at[j],
        )

    for j in range(m):
        w_copy(j).start()

    barrier = pltpu.get_barrier_semaphore()
    for step in range(1, m):
        other = lax.rem(hz + step, m)
        pl.semaphore_signal(barrier, inc=1, device_id=(me, other), device_id_type=MESH)

    def greet(step, carry):
        other = lax.rem(me + step, n)
        pl.semaphore_signal(barrier, inc=1, device_id=(other, hz), device_id_type=MESH)
        return carry

    lax.fori_loop(1, n, greet, 0)

    kv[me] = jnp.concatenate([k_ref[...], v_ref[...]], axis=0).T
    pl.semaphore_wait(barrier, n - 1 + m - 1)

    def seq_copy(buf, send, recv, slot, dst):
        return pltpu.make_async_remote_copy(
            src_ref=buf.at[slot], dst_ref=buf.at[slot],
            send_sem=send.at[dst], recv_sem=recv.at[slot],
            device_id=(dst, hz), device_id_type=MESH,
        )

    def pass_on(buf, send, recv, slot):
        return pltpu.make_async_remote_copy(
            src_ref=buf.at[slot], dst_ref=buf.at[slot],
            send_sem=send.at[slot], recv_sem=recv.at[slot],
            device_id=(sibling, hz), device_id_type=MESH,
        )

    @pl.when(parity == 0)
    def _():
        seq_copy(kv, kv_send, kv_recv, me, sibling).start()

    def send_kv(i, carry):
        seq_copy(kv, kv_send, kv_recv, me, 2 * i + parity).start()
        return carry

    lax.fori_loop(pair + 1, n // 2, send_kv, 0)

    for j in range(m):
        w_copy(j).wait()

    def share(j):
        return nt(wpad[j, pad:pad + width, :], og_ref[...])

    def part_copy(dst):
        return pltpu.make_async_remote_copy(
            src_ref=part.at[dst], dst_ref=got.at[hz],
            send_sem=pg_send.at[dst], recv_sem=pg_recv.at[hz],
            device_id=(me, dst), device_id_type=MESH,
        )

    for step in range(1, m):
        other = lax.rem(hz + step, m)
        part[other] = share(other).astype(jnp.bfloat16)
        part_copy(other).start()
    own_share = share(hz)

    lane = lax.broadcasted_iota(jnp.int32, (rows, wide), 1)

    def low_mask(h):
        return (lane >= h * HD) & (lane < (h + 1) * HD)

    def high_mask(h):
        return (lane >= pad + h * HD) & (lane < pad + (h + 1) * HD)

    q_wide = jnp.concatenate([q_ref[...], jnp.zeros((pad, rows), jnp.bfloat16)], axis=0).T
    zero_16 = jnp.zeros((rows, wide), jnp.bfloat16)
    own_k = kv[me][:, low]
    own_v = kv[me][:, high]
    for h in range(heads):
        qm[h] = jnp.where(low_mask(h), q_wide, zero_16)
        km[h] = jnp.where(low_mask(h), own_k, zero_16)
        vm[h] = jnp.where(high_mask(h), own_v, zero_16)

    row_id = lax.broadcasted_iota(jnp.int32, (rows, rows), 0)
    col_id = lax.broadcasted_iota(jnp.int32, (rows, rows), 1)

    for h in range(heads):
        s = nt(qm[h], own_k) * factor
        s = jnp.where(col_id <= row_id, s, masked_score)
        top = jnp.max(s, axis=1, keepdims=True)
        e = jnp.exp2(s - top)
        max_s[h] = top
        sum_s[h] = jnp.sum(e, axis=1, keepdims=True)
        acc_a[h] = nn(e.astype(jnp.bfloat16), own_v)

    total = own_share
    for step in range(1, m):
        other = lax.rem(hz + step, m)
        pltpu.make_async_remote_copy(
            src_ref=part.at[other], dst_ref=got.at[other],
            send_sem=pg_send.at[other], recv_sem=pg_recv.at[other],
            device_id=(me, other), device_id_type=MESH,
        ).wait_recv()
        total = total + got[other].astype(jnp.float32)
    qd[me] = jnp.concatenate([q_ref[...], total.astype(jnp.bfloat16)], axis=0).T

    @pl.when(parity == 1)
    def _():
        seq_copy(qd, qd_send, qd_recv, me, sibling).start()

    def send_qd(i, carry):
        seq_copy(qd, qd_send, qd_recv, me, 2 * (pair - 1 - i) + parity).start()
        return carry

    lax.fori_loop(0, pair, send_qd, 0)
    own_g = qd[me][:, high]
    for h in range(heads):
        dom[h] = jnp.where(high_mask(h), own_g, zero_16)

    def forward(i, carry):
        turn = i - parity + 2
        same = (turn >= 2) & (lax.rem(turn, 2) == 0)
        j = 2 * (pair - lax.div(turn, 2)) + jnp.where(lax.rem(turn, 2) == 0, parity, 1 - parity)
        seq_copy(kv, kv_send, kv_recv, j, me).wait_recv()

        @pl.when(same)
        def _():
            pass_on(kv, kv_pass, kv_recv, j).start()

        block = kv.at[j]
        for h in range(heads):
            s = nt(qm[h], block[:, low]) * factor
            old = max_s[h]
            top = jnp.maximum(old, jnp.max(s, axis=1, keepdims=True))
            alpha = jnp.exp2(old - top)
            e = jnp.exp2(s - top)
            max_s[h] = top
            sum_s[h] = sum_s[h] * alpha + jnp.sum(e, axis=1, keepdims=True)
            acc_a[h] = acc_a[h] * alpha + nn(e.astype(jnp.bfloat16), block[:, high])
        return carry

    lax.fori_loop(0, me, forward, 0)

    mixed = jnp.zeros((rows, wide), jnp.float32)
    for h in range(heads):
        mixed = jnp.where(high_mask(h), acc_a[h] * (1.0 / sum_s[h]), mixed)
    attended = mixed.astype(jnp.bfloat16).astype(jnp.float32)
    upper = attended[:half, pad:]
    lower = attended[half:, pad:]
    att[hz] = jnp.concatenate([upper, lower], axis=1).astype(jnp.bfloat16)

    def att_copy(slot, dst):
        return pltpu.make_async_remote_copy(
            src_ref=att.at[slot], dst_ref=att.at[slot],
            send_sem=at_send.at[dst], recv_sem=at_recv.at[slot],
            device_id=(me, dst), device_id_type=MESH,
        )

    for step in range(1, m):
        att_copy(hz, lax.rem(hz + step, m)).start()

    product = attended * own_g.astype(jnp.float32)
    stat_lane = lax.broadcasted_iota(jnp.int32, (rows, 128), 1)
    stats = jnp.zeros((rows, 128), jnp.float32)
    for h in range(heads):
        row_dot = jnp.sum(jnp.where(high_mask(h), product, 0.0), axis=1, keepdims=True)
        log_total = max_s[h] + jnp.log2(sum_s[h])
        max_s[h] = log_total
        dot_s[h] = row_dot
        stats = jnp.where(stat_lane == h, log_total, stats)
        stats = jnp.where(stat_lane == heads + h, row_dot, stats)
    lr[me] = stats.T[:stat_rows, :]

    def send_lr(j, carry):
        seq_copy(lr, lr_send, lr_recv, me, j).start()
        return carry

    lax.fori_loop(0, me, send_lr, 0)

    def query_step(block, h, own):
        s = nt(qm[h], block[:, low]) * factor
        if own:
            s = jnp.where(col_id <= row_id, s, masked_score)
        p = jnp.exp2(s - max_s[h])
        ds = p * (nt(dom[h], block[:, high]) - dot_s[h])
        return nn(ds.astype(jnp.bfloat16), block[:, low])

    for h in range(heads):
        acc_a[h] = query_step(kv.at[me], h, True)

    def query_loop(i, carry):
        block = kv.at[i]
        for h in range(heads):
            acc_a[h] = acc_a[h] + query_step(block, h, False)
        return carry

    lax.fori_loop(0, me, query_loop, 0)
    query_sum = jnp.zeros((rows, wide), jnp.float32)
    for h in range(heads):
        query_sum = jnp.where(low_mask(h), acc_a[h], query_sum)
    qg_ref[...] = (query_sum * scale).T[:width, :].astype(jnp.bfloat16)

    def key_step(block, stat, h, own):
        s = nt(km[h], block[:, low]) * factor
        if own:
            s = jnp.where(row_id <= col_id, s, masked_score)
        p = jnp.exp2(s - stat[h:h + 1, :])
        value_part = nn(p.astype(jnp.bfloat16), block[:, high])
        ds = p * (nt(vm[h], block[:, high]) - stat[heads + h:heads + h + 1, :])
        return nn(ds.astype(jnp.bfloat16), block[:, low]), value_part

    for h in range(heads):
        acc_b[h], acc_c[h] = key_step(qd.at[me], lr.at[me], h, True)

    wpad[:, 0:pad, :] = jnp.zeros((m, pad, cols), jnp.bfloat16)
    wpad[:, pad + width:, :] = jnp.zeros((m, pad, cols), jnp.bfloat16)

    def project(slot):
        block = att.at[slot]
        return (
            nn(block[:, low], wpad[slot, pad:, :]),
            nn(block[:, high], wpad[slot, :wide, :]),
        )

    proj_top, proj_low = project(hz)
    for step in range(1, m):
        other = lax.rem(hz + step, m)
        att_copy(other, hz).wait_recv()
        more_top, more_low = project(other)
        proj_top = proj_top + more_top
        proj_low = proj_low + more_low
    proj_ref[:half, :] = proj_top.astype(jnp.bfloat16)
    proj_ref[half:, :] = proj_low.astype(jnp.bfloat16)

    def key_loop(i, carry):
        turn = i - (1 - parity) + 2
        same = (turn >= 2) & (lax.rem(turn, 2) == 0)
        j = 2 * (pair + lax.div(turn, 2)) + jnp.where(lax.rem(turn, 2) == 0, parity, 1 - parity)
        seq_copy(qd, qd_send, qd_recv, j, me).wait_recv()

        @pl.when(same)
        def _():
            pass_on(qd, qd_pass, qd_recv, j).start()

        seq_copy(lr, lr_send, lr_recv, j, me).wait_recv()
        for h in range(heads):
            key_part, value_part = key_step(qd.at[j], lr.at[j], h, False)
            acc_b[h] = acc_b[h] + key_part
            acc_c[h] = acc_c[h] + value_part
        return carry

    lax.fori_loop(0, n - 1 - me, key_loop, 0)
    key_sum = jnp.zeros((rows, wide), jnp.float32)
    value_sum = jnp.zeros((rows, wide), jnp.float32)
    for h in range(heads):
        key_sum = jnp.where(low_mask(h), acc_b[h], key_sum)
        value_sum = jnp.where(high_mask(h), acc_c[h], value_sum)
    kg_ref[...] = (key_sum * scale).T[:width, :].astype(jnp.bfloat16)
    vg_ref[...] = value_sum.T[pad:, :].astype(jnp.bfloat16)

    @pl.when(parity == 0)
    def _():
        seq_copy(kv, kv_send, kv_recv, me, sibling).wait_send()

    @pl.when(parity == 1)
    def _():
        seq_copy(qd, qd_send, qd_recv, me, sibling).wait_send()

    def sent_later(i, carry):
        seq_copy(kv, kv_send, kv_recv, me, 2 * i + parity).wait_send()
        pass_on(qd, qd_pass, qd_recv, 2 * i + parity).wait_send()
        return carry

    lax.fori_loop(pair + 1, n // 2, sent_later, 0)

    def sent_earlier(i, carry):
        seq_copy(qd, qd_send, qd_recv, me, 2 * i + parity).wait_send()
        pass_on(kv, kv_pass, kv_recv, 2 * i + parity).wait_send()
        return carry

    lax.fori_loop(0, pair, sent_earlier, 0)

    def sent_lr(j, carry):
        seq_copy(lr, lr_send, lr_recv, me, j).wait_send()
        return carry

    lax.fori_loop(0, me, sent_lr, 0)
    for step in range(1, m):
        other = lax.rem(hz + step, m)
        part_copy(other).wait_send()
        att_copy(hz, other).wait_send()


def finish(*refs):
    count = len(refs) // 2
    for source, target in zip(refs[:count], refs[count:]):
        target[...] = source[...]


def per_device(n, m, queries, keys, values, out_weight, out_grad):
    rows, width = queries.shape
    cols = out_grad.shape[1]
    heads = width // HD
    wide = round_up(width, 128)
    pad = wide - width
    stat_rows = round_up(2 * heads, 8)
    bf16, f32 = jnp.bfloat16, jnp.float32
    in_vmem = pl.BlockSpec(memory_space=pltpu.VMEM)
    dma = pltpu.SemaphoreType.DMA
    macs = rows * rows * n * 9 * width + 2 * rows * width * m * cols
    shapes = (
        jax.ShapeDtypeStruct((rows, cols), bf16),
        jax.ShapeDtypeStruct((width, rows), bf16),
        jax.ShapeDtypeStruct((width, rows), bf16),
        jax.ShapeDtypeStruct((width, rows), bf16),
    )
    results = pl.pallas_call(
        functools.partial(kernel, n, m),
        out_shape=shapes,
        in_specs=[in_vmem, in_vmem, in_vmem, pl.BlockSpec(memory_space=pl.ANY), in_vmem],
        out_specs=(in_vmem,) * 4,
        scratch_shapes=[
            pltpu.VMEM((n, rows, 2 * width), bf16),
            pltpu.VMEM((n, rows, 2 * width), bf16),
            pltpu.VMEM((n, stat_rows, rows), f32),
            pltpu.VMEM((m, width, rows), bf16),
            pltpu.VMEM((m, width, rows), bf16),
            pltpu.VMEM((m, rows // 2, 2 * width), bf16),
            pltpu.VMEM((m, pad + width + pad, cols), bf16),
        ]
        + [pltpu.VMEM((heads, rows, wide), bf16)] * 4
        + [pltpu.VMEM((heads, rows, wide), f32)] * 3
        + [pltpu.VMEM((heads, rows, 1), f32)] * 3
        + [dma((m,))]
        + [dma((n,))] * 6
        + [dma((m,))] * 4
        + [dma((n,))] * 2,
        compiler_params=pltpu.CompilerParams(
            collective_id=0, has_side_effects=True, vmem_limit_bytes=56 * 1024 * 1024
        ),
        cost_estimate=pl.CostEstimate(
            flops=macs, bytes_accessed=6 * rows * width * 2, transcendentals=rows * rows * n * heads
        ),
    )(queries.T, keys.T, values.T, out_weight, out_grad)
    projected, query_grad, key_grad, value_grad = pl.pallas_call(
        finish, out_shape=shapes, in_specs=[in_vmem] * 4, out_specs=(in_vmem,) * 4
    )(*results)
    return projected, query_grad.T, key_grad.T, value_grad.T


def solution(mesh):
    return jax.shard_map(
        functools.partial(per_device, mesh.shape["seq"], mesh.shape["head"]),
        mesh=mesh,
        in_specs=(P("seq", "head"), P("seq", "head"), P("seq", "head"), P(), P("seq", "head")),
        out_specs=(P("seq", "head"), P("seq", "head"), P("seq", "head"), P("seq", "head")),
        check_vma=False,
    )
```

```python
import functools
import math

import jax
import jax.numpy as jnp
from jax import lax
from jax.experimental import pallas as pl
from jax.experimental.pallas import tpu as pltpu
from jax.sharding import PartitionSpec as P

HD = 64
MESH = pl.DeviceIdType.MESH
masked_score = -1e30


def round_up(value, unit):
    return -(-value // unit) * unit


def nt(left, right):
    return lax.dot_general(
        left, right, (((1,), (1,)), ((), ())), preferred_element_type=jnp.float32
    )


def nn(left, right):
    return jnp.dot(left, right, preferred_element_type=jnp.float32)


def kernel(
    n, m, q_ref, k_ref, v_ref, w_ref, og_ref,
    proj_ref, qg_ref, kg_ref, vg_ref,
    kv, qd, lr, part, got, att, wpad, qm, dom, km, vm,
    acc_a, acc_b, acc_c, max_s, sum_s, dot_s,
    w_sem, kv_send, kv_recv, qd_send, qd_recv, lr_send, lr_recv,
    pg_send, pg_recv, at_send, at_recv, kv_pass, qd_pass,
):
    width, rows = q_ref.shape
    cols = og_ref.shape[1]
    heads = width // HD
    wide = round_up(width, 128)
    pad = wide - width
    low = slice(0, wide)
    high = slice(2 * width - wide, 2 * width)
    half = rows // 2
    stat_rows = lr.shape[1]
    scale = HD ** (-0.5)
    factor = scale / math.log(2.0)
    me = lax.axis_index("seq")
    hz = lax.axis_index("head")
    parity = lax.rem(me, 2)
    pair = lax.div(me, 2)
    sibling = 2 * pair + 1 - parity

    def w_copy(j):
        return pltpu.make_async_copy(
            w_ref.at[pl.ds(j * width, width), pl.ds(pl.multiple_of(hz * cols, 128), cols)],
            wpad.at[j, pl.ds(pad, width), :],
            w_sem.at[j],
        )

    for j in range(m):
        w_copy(j).start()

    barrier = pltpu.get_barrier_semaphore()
    for step in range(1, m):
        other = lax.rem(hz + step, m)
        pl.semaphore_signal(barrier, inc=1, device_id=(me, other), device_id_type=MESH)

    def greet(step, carry):
        other = lax.rem(me + step, n)
        pl.semaphore_signal(barrier, inc=1, device_id=(other, hz), device_id_type=MESH)
        return carry

    lax.fori_loop(1, n, greet, 0)

    kv[me] = jnp.concatenate([k_ref[...], v_ref[...]], axis=0).T
    pl.semaphore_wait(barrier, n - 1 + m - 1)

    def seq_copy(buf, send, recv, slot, dst):
        return pltpu.make_async_remote_copy(
            src_ref=buf.at[slot], dst_ref=buf.at[slot],
            send_sem=send.at[dst], recv_sem=recv.at[slot],
            device_id=(dst, hz), device_id_type=MESH,
        )

    def pass_on(buf, send, recv, slot):
        return pltpu.make_async_remote_copy(
            src_ref=buf.at[slot], dst_ref=buf.at[slot],
            send_sem=send.at[slot], recv_sem=recv.at[slot],
            device_id=(sibling, hz), device_id_type=MESH,
        )

    @pl.when(parity == 0)
    def _():
        seq_copy(kv, kv_send, kv_recv, me, sibling).start()

    def send_kv(i, carry):
        seq_copy(kv, kv_send, kv_recv, me, 2 * i + parity).start()
        return carry

    lax.fori_loop(pair + 1, n // 2, send_kv, 0)

    for j in range(m):
        w_copy(j).wait()

    def share(j):
        return nt(wpad[j, pad:pad + width, :], og_ref[...])

    def part_copy(dst):
        return pltpu.make_async_remote_copy(
            src_ref=part.at[dst], dst_ref=got.at[hz],
            send_sem=pg_send.at[dst], recv_sem=pg_recv.at[hz],
            device_id=(me, dst), device_id_type=MESH,
        )

    for step in range(1, m):
        other = lax.rem(hz + step, m)
        part[other] = share(other).astype(jnp.bfloat16)
        part_copy(other).start()
    own_share = share(hz)

    lane = lax.broadcasted_iota(jnp.int32, (rows, wide), 1)

    def low_mask(h):
        return (lane >= h * HD) & (lane < (h + 1) * HD)

    def high_mask(h):
        return (lane >= pad + h * HD) & (lane < pad + (h + 1) * HD)

    q_wide = jnp.concatenate([q_ref[...], jnp.zeros((pad, rows), jnp.bfloat16)], axis=0).T
    zero_16 = jnp.zeros((rows, wide), jnp.bfloat16)
    own_k = kv[me][:, low]
    own_v = kv[me][:, high]
    for h in range(heads):
        qm[h] = jnp.where(low_mask(h), q_wide, zero_16)
        km[h] = jnp.where(low_mask(h), own_k, zero_16)
        vm[h] = jnp.where(high_mask(h), own_v, zero_16)

    row_id = lax.broadcasted_iota(jnp.int32, (rows, rows), 0)
    col_id = lax.broadcasted_iota(jnp.int32, (rows, rows), 1)

    one_16 = jnp.ones((rows, wide), jnp.bfloat16)

    def with_ones(block):
        return jnp.where(lane < pad, one_16, block)

    own_ones = with_ones(own_v)
    for h in range(heads):
        s = nt(qm[h], own_k) * factor
        s = jnp.where(col_id <= row_id, s, masked_score)
        top = jnp.max(s, axis=1, keepdims=True)
        e = jnp.exp2(s - top)
        max_s[h] = top
        acc_a[h] = nn(e.astype(jnp.bfloat16), own_ones)

    def forward(i, carry):
        turn = i - parity + 2
        same = (turn >= 2) & (lax.rem(turn, 2) == 0)
        j = 2 * (pair - lax.div(turn, 2)) + jnp.where(lax.rem(turn, 2) == 0, parity, 1 - parity)
        seq_copy(kv, kv_send, kv_recv, j, me).wait_recv()

        @pl.when(same)
        def _():
            pass_on(kv, kv_pass, kv_recv, j).start()

        block = kv.at[j]
        value_ones = with_ones(block[:, high])
        for h in range(heads):
            s = nt(qm[h], block[:, low]) * factor
            old = max_s[h]
            top = jnp.maximum(old, jnp.max(s, axis=1, keepdims=True))
            alpha = jnp.exp2(old - top)
            e = jnp.exp2(s - top)
            max_s[h] = top
            acc_a[h] = acc_a[h] * alpha + nn(e.astype(jnp.bfloat16), value_ones)
        return carry

    lax.fori_loop(0, me, forward, 0)

    mixed = jnp.zeros((rows, wide), jnp.float32)
    for h in range(heads):
        sum_s[h] = acc_a[h][:, 0:1]
        mixed = jnp.where(high_mask(h), acc_a[h] * (1.0 / sum_s[h]), mixed)
    attended = mixed.astype(jnp.bfloat16).astype(jnp.float32)
    upper = attended[:half, pad:]
    lower = attended[half:, pad:]
    att[hz] = jnp.concatenate([upper, lower], axis=1).astype(jnp.bfloat16)

    def att_copy(slot, dst):
        return pltpu.make_async_remote_copy(
            src_ref=att.at[slot], dst_ref=att.at[slot],
            send_sem=at_send.at[dst], recv_sem=at_recv.at[slot],
            device_id=(me, dst), device_id_type=MESH,
        )

    for step in range(1, m):
        att_copy(hz, lax.rem(hz + step, m)).start()

    total = own_share
    for step in range(1, m):
        other = lax.rem(hz + step, m)
        pltpu.make_async_remote_copy(
            src_ref=part.at[other], dst_ref=got.at[other],
            send_sem=pg_send.at[other], recv_sem=pg_recv.at[other],
            device_id=(me, other), device_id_type=MESH,
        ).wait_recv()
        total = total + got[other].astype(jnp.float32)
    qd[me] = jnp.concatenate([q_ref[...], total.astype(jnp.bfloat16)], axis=0).T

    @pl.when(parity == 1)
    def _():
        seq_copy(qd, qd_send, qd_recv, me, sibling).start()

    def send_qd(i, carry):
        seq_copy(qd, qd_send, qd_recv, me, 2 * (pair - 1 - i) + parity).start()
        return carry

    lax.fori_loop(0, pair, send_qd, 0)
    own_g = qd[me][:, high]
    for h in range(heads):
        dom[h] = jnp.where(high_mask(h), own_g, zero_16)

    product = attended * own_g.astype(jnp.float32)
    stat_lane = lax.broadcasted_iota(jnp.int32, (rows, 128), 1)
    stats = jnp.zeros((rows, 128), jnp.float32)
    for h in range(heads):
        row_dot = jnp.sum(jnp.where(high_mask(h), product, 0.0), axis=1, keepdims=True)
        log_total = max_s[h] + jnp.log2(sum_s[h])
        max_s[h] = log_total
        dot_s[h] = row_dot
        stats = jnp.where(stat_lane == h, log_total, stats)
        stats = jnp.where(stat_lane == heads + h, row_dot, stats)
    lr[me] = stats.T[:stat_rows, :]

    def send_lr(j, carry):
        seq_copy(lr, lr_send, lr_recv, me, j).start()
        return carry

    lax.fori_loop(0, me, send_lr, 0)

    def query_step(block, h, own):
        s = nt(qm[h], block[:, low]) * factor
        if own:
            s = jnp.where(col_id <= row_id, s, masked_score)
        p = jnp.exp2(s - max_s[h])
        ds = p * (nt(dom[h], block[:, high]) - dot_s[h])
        return nn(ds.astype(jnp.bfloat16), block[:, low])

    for h in range(heads):
        acc_a[h] = query_step(kv.at[me], h, True)

    def query_loop(i, carry):
        block = kv.at[i]
        for h in range(heads):
            acc_a[h] = acc_a[h] + query_step(block, h, False)
        return carry

    lax.fori_loop(0, me, query_loop, 0)
    query_sum = jnp.zeros((rows, wide), jnp.float32)
    for h in range(heads):
        query_sum = jnp.where(low_mask(h), acc_a[h], query_sum)
    qg_ref[...] = (query_sum * scale).T[:width, :].astype(jnp.bfloat16)

    def key_step(block, stat, h, own):
        s = nt(km[h], block[:, low]) * factor
        if own:
            s = jnp.where(row_id <= col_id, s, masked_score)
        p = jnp.exp2(s - stat[h:h + 1, :])
        value_part = nn(p.astype(jnp.bfloat16), block[:, high])
        ds = p * (nt(vm[h], block[:, high]) - stat[heads + h:heads + h + 1, :])
        return nn(ds.astype(jnp.bfloat16), block[:, low]), value_part

    for h in range(heads):
        acc_b[h], acc_c[h] = key_step(qd.at[me], lr.at[me], h, True)

    wpad[:, 0:pad, :] = jnp.zeros((m, pad, cols), jnp.bfloat16)
    wpad[:, pad + width:, :] = jnp.zeros((m, pad, cols), jnp.bfloat16)

    def project(slot):
        block = att.at[slot]
        return (
            nn(block[:, low], wpad[slot, pad:, :]),
            nn(block[:, high], wpad[slot, :wide, :]),
        )

    proj_top, proj_low = project(hz)
    for step in range(1, m):
        other = lax.rem(hz + step, m)
        att_copy(other, hz).wait_recv()
        more_top, more_low = project(other)
        proj_top = proj_top + more_top
        proj_low = proj_low + more_low
    proj_ref[:half, :] = proj_top.astype(jnp.bfloat16)
    proj_ref[half:, :] = proj_low.astype(jnp.bfloat16)

    def key_loop(i, carry):
        turn = i - (1 - parity) + 2
        same = (turn >= 2) & (lax.rem(turn, 2) == 0)
        j = 2 * (pair + lax.div(turn, 2)) + jnp.where(lax.rem(turn, 2) == 0, parity, 1 - parity)
        seq_copy(qd, qd_send, qd_recv, j, me).wait_recv()

        @pl.when(same)
        def _():
            pass_on(qd, qd_pass, qd_recv, j).start()

        seq_copy(lr, lr_send, lr_recv, j, me).wait_recv()
        for h in range(heads):
            key_part, value_part = key_step(qd.at[j], lr.at[j], h, False)
            acc_b[h] = acc_b[h] + key_part
            acc_c[h] = acc_c[h] + value_part
        return carry

    lax.fori_loop(0, n - 1 - me, key_loop, 0)
    key_sum = jnp.zeros((rows, wide), jnp.float32)
    value_sum = jnp.zeros((rows, wide), jnp.float32)
    for h in range(heads):
        key_sum = jnp.where(low_mask(h), acc_b[h], key_sum)
        value_sum = jnp.where(high_mask(h), acc_c[h], value_sum)
    kg_ref[...] = (key_sum * scale).T[:width, :].astype(jnp.bfloat16)
    vg_ref[...] = value_sum.T[pad:, :].astype(jnp.bfloat16)

    @pl.when(parity == 0)
    def _():
        seq_copy(kv, kv_send, kv_recv, me, sibling).wait_send()

    @pl.when(parity == 1)
    def _():
        seq_copy(qd, qd_send, qd_recv, me, sibling).wait_send()

    def sent_later(i, carry):
        seq_copy(kv, kv_send, kv_recv, me, 2 * i + parity).wait_send()
        pass_on(qd, qd_pass, qd_recv, 2 * i + parity).wait_send()
        return carry

    lax.fori_loop(pair + 1, n // 2, sent_later, 0)

    def sent_earlier(i, carry):
        seq_copy(qd, qd_send, qd_recv, me, 2 * i + parity).wait_send()
        pass_on(kv, kv_pass, kv_recv, 2 * i + parity).wait_send()
        return carry

    lax.fori_loop(0, pair, sent_earlier, 0)

    def sent_lr(j, carry):
        seq_copy(lr, lr_send, lr_recv, me, j).wait_send()
        return carry

    lax.fori_loop(0, me, sent_lr, 0)
    for step in range(1, m):
        other = lax.rem(hz + step, m)
        part_copy(other).wait_send()
        att_copy(hz, other).wait_send()


def finish(*refs):
    count = len(refs) // 2
    for source, target in zip(refs[:count], refs[count:]):
        target[...] = source[...]


def per_device(n, m, queries, keys, values, out_weight, out_grad):
    rows, width = queries.shape
    cols = out_grad.shape[1]
    heads = width // HD
    wide = round_up(width, 128)
    pad = wide - width
    stat_rows = round_up(2 * heads, 8)
    bf16, f32 = jnp.bfloat16, jnp.float32
    in_vmem = pl.BlockSpec(memory_space=pltpu.VMEM)
    dma = pltpu.SemaphoreType.DMA
    macs = rows * rows * n * 9 * width + 2 * rows * width * m * cols
    shapes = (
        jax.ShapeDtypeStruct((rows, cols), bf16),
        jax.ShapeDtypeStruct((width, rows), bf16),
        jax.ShapeDtypeStruct((width, rows), bf16),
        jax.ShapeDtypeStruct((width, rows), bf16),
    )
    results = pl.pallas_call(
        functools.partial(kernel, n, m),
        out_shape=shapes,
        in_specs=[in_vmem, in_vmem, in_vmem, pl.BlockSpec(memory_space=pl.ANY), in_vmem],
        out_specs=(in_vmem,) * 4,
        scratch_shapes=[
            pltpu.VMEM((n, rows, 2 * width), bf16),
            pltpu.VMEM((n, rows, 2 * width), bf16),
            pltpu.VMEM((n, stat_rows, rows), f32),
            pltpu.VMEM((m, width, rows), bf16),
            pltpu.VMEM((m, width, rows), bf16),
            pltpu.VMEM((m, rows // 2, 2 * width), bf16),
            pltpu.VMEM((m, pad + width + pad, cols), bf16),
        ]
        + [pltpu.VMEM((heads, rows, wide), bf16)] * 4
        + [pltpu.VMEM((heads, rows, wide), f32)] * 3
        + [pltpu.VMEM((heads, rows, 1), f32)] * 3
        + [dma((m,))]
        + [dma((n,))] * 6
        + [dma((m,))] * 4
        + [dma((n,))] * 2,
        compiler_params=pltpu.CompilerParams(
            collective_id=0, has_side_effects=True, vmem_limit_bytes=56 * 1024 * 1024
        ),
        cost_estimate=pl.CostEstimate(
            flops=macs, bytes_accessed=6 * rows * width * 2, transcendentals=rows * rows * n * heads
        ),
    )(queries.T, keys.T, values.T, out_weight, out_grad)
    projected, query_grad, key_grad, value_grad = pl.pallas_call(
        finish, out_shape=shapes, in_specs=[in_vmem] * 4, out_specs=(in_vmem,) * 4
    )(*results)
    return projected, query_grad.T, key_grad.T, value_grad.T


def solution(mesh):
    return jax.shard_map(
        functools.partial(per_device, mesh.shape["seq"], mesh.shape["head"]),
        mesh=mesh,
        in_specs=(P("seq", "head"), P("seq", "head"), P("seq", "head"), P(), P("seq", "head")),
        out_specs=(P("seq", "head"), P("seq", "head"), P("seq", "head"), P("seq", "head")),
        check_vma=False,
    )
```

```python
import functools
import math

import jax
import jax.numpy as jnp
from jax import lax
from jax.experimental import pallas as pl
from jax.experimental.pallas import tpu as pltpu
from jax.sharding import PartitionSpec as P

HD = 64
MESH = pl.DeviceIdType.MESH
masked_score = -1e30


def round_up(value, unit):
    return -(-value // unit) * unit


def nt(left, right):
    return lax.dot_general(
        left, right, (((1,), (1,)), ((), ())), preferred_element_type=jnp.float32
    )


def nn(left, right):
    return jnp.dot(left, right, preferred_element_type=jnp.float32)


def kernel(
    n, m, q_ref, k_ref, v_ref, w_ref, og_ref,
    proj_ref, qg_ref, kg_ref, vg_ref,
    kv, qd, lr, part, got, att, wpad, qm, dom, km, vm,
    acc_a, acc_b, acc_c, max_s, sum_s, dot_s,
    w_sem, kv_send, kv_recv, qd_send, qd_recv, lr_send, lr_recv,
    pg_send, pg_recv, at_send, at_recv, kv_pass, qd_pass,
):
    width, rows = q_ref.shape
    cols = og_ref.shape[1]
    heads = width // HD
    wide = round_up(width, 128)
    pad = wide - width
    low = slice(0, wide)
    high = slice(2 * width - wide, 2 * width)
    half = rows // 2
    stat_rows = lr.shape[1]
    scale = HD ** (-0.5)
    factor = scale / math.log(2.0)
    me = lax.axis_index("seq")
    hz = lax.axis_index("head")
    parity = lax.rem(me, 2)
    pair = lax.div(me, 2)
    sibling = 2 * pair + 1 - parity

    def w_copy(j):
        return pltpu.make_async_copy(
            w_ref.at[pl.ds(j * width, width), pl.ds(pl.multiple_of(hz * cols, 128), cols)],
            wpad.at[j, pl.ds(pad, width), :],
            w_sem.at[j],
        )

    for j in range(m):
        w_copy(j).start()

    barrier = pltpu.get_barrier_semaphore()
    for step in range(1, m):
        other = lax.rem(hz + step, m)
        pl.semaphore_signal(barrier, inc=1, device_id=(me, other), device_id_type=MESH)

    def greet(step, carry):
        other = lax.rem(me + step, n)
        pl.semaphore_signal(barrier, inc=1, device_id=(other, hz), device_id_type=MESH)
        return carry

    lax.fori_loop(1, n, greet, 0)

    kv[me] = jnp.concatenate([k_ref[...], v_ref[...]], axis=0).T

    def seq_copy(buf, send, recv, slot, dst):
        return pltpu.make_async_remote_copy(
            src_ref=buf.at[slot], dst_ref=buf.at[slot],
            send_sem=send.at[dst], recv_sem=recv.at[slot],
            device_id=(dst, hz), device_id_type=MESH,
        )

    def pass_on(buf, send, recv, slot):
        return pltpu.make_async_remote_copy(
            src_ref=buf.at[slot], dst_ref=buf.at[slot],
            send_sem=send.at[slot], recv_sem=recv.at[slot],
            device_id=(sibling, hz), device_id_type=MESH,
        )

    for j in range(m):
        w_copy(j).wait()

    def share(j):
        return nt(wpad[j, pad:pad + width, :], og_ref[...])

    def part_copy(dst):
        return pltpu.make_async_remote_copy(
            src_ref=part.at[dst], dst_ref=got.at[hz],
            send_sem=pg_send.at[dst], recv_sem=pg_recv.at[hz],
            device_id=(me, dst), device_id_type=MESH,
        )

    for step in range(1, m):
        other = lax.rem(hz + step, m)
        part[other] = share(other).astype(jnp.bfloat16)

    pl.semaphore_wait(barrier, n - 1 + m - 1)
    @pl.when(parity == 0)
    def _():
        seq_copy(kv, kv_send, kv_recv, me, sibling).start()

    def send_kv(i, carry):
        seq_copy(kv, kv_send, kv_recv, me, 2 * i + parity).start()
        return carry

    lax.fori_loop(pair + 1, n // 2, send_kv, 0)

    for step in range(1, m):
        part_copy(lax.rem(hz + step, m)).start()
    own_share = share(hz)

    lane = lax.broadcasted_iota(jnp.int32, (rows, wide), 1)

    def low_mask(h):
        return (lane >= h * HD) & (lane < (h + 1) * HD)

    def high_mask(h):
        return (lane >= pad + h * HD) & (lane < pad + (h + 1) * HD)

    q_wide = jnp.concatenate([q_ref[...], jnp.zeros((pad, rows), jnp.bfloat16)], axis=0).T
    zero_16 = jnp.zeros((rows, wide), jnp.bfloat16)
    own_k = kv[me][:, low]
    own_v = kv[me][:, high]
    for h in range(heads):
        qm[h] = jnp.where(low_mask(h), q_wide, zero_16)
        km[h] = jnp.where(low_mask(h), own_k, zero_16)
        vm[h] = jnp.where(high_mask(h), own_v, zero_16)

    row_id = lax.broadcasted_iota(jnp.int32, (rows, rows), 0)
    col_id = lax.broadcasted_iota(jnp.int32, (rows, rows), 1)

    one_16 = jnp.ones((rows, wide), jnp.bfloat16)

    def with_ones(block):
        return jnp.where(lane < pad, one_16, block)

    own_ones = with_ones(own_v)
    for h in range(heads):
        s = nt(qm[h], own_k) * factor
        s = jnp.where(col_id <= row_id, s, masked_score)
        top = jnp.max(s, axis=1, keepdims=True)
        e = jnp.exp2(s - top)
        max_s[h] = top
        acc_a[h] = nn(e.astype(jnp.bfloat16), own_ones)

    def forward(i, carry):
        turn = i - parity + 2
        same = (turn >= 2) & (lax.rem(turn, 2) == 0)
        j = 2 * (pair - lax.div(turn, 2)) + jnp.where(lax.rem(turn, 2) == 0, parity, 1 - parity)
        seq_copy(kv, kv_send, kv_recv, j, me).wait_recv()

        @pl.when(same)
        def _():
            pass_on(kv, kv_pass, kv_recv, j).start()

        block = kv.at[j]
        value_ones = with_ones(block[:, high])
        for h in range(heads):
            s = nt(qm[h], block[:, low]) * factor
            old = max_s[h]
            top = jnp.maximum(old, jnp.max(s, axis=1, keepdims=True))
            alpha = jnp.exp2(old - top)
            e = jnp.exp2(s - top)
            max_s[h] = top
            acc_a[h] = acc_a[h] * alpha + nn(e.astype(jnp.bfloat16), value_ones)
        return carry

    lax.fori_loop(0, me, forward, 0)

    mixed = jnp.zeros((rows, wide), jnp.float32)
    for h in range(heads):
        sum_s[h] = acc_a[h][:, 0:1]
        mixed = jnp.where(high_mask(h), acc_a[h] * (1.0 / sum_s[h]), mixed)
    attended = mixed.astype(jnp.bfloat16).astype(jnp.float32)
    upper = attended[:half, pad:]
    lower = attended[half:, pad:]
    att[hz] = jnp.concatenate([upper, lower], axis=1).astype(jnp.bfloat16)

    def att_copy(slot, dst):
        return pltpu.make_async_remote_copy(
            src_ref=att.at[slot], dst_ref=att.at[slot],
            send_sem=at_send.at[dst], recv_sem=at_recv.at[slot],
            device_id=(me, dst), device_id_type=MESH,
        )

    for step in range(1, m):
        att_copy(hz, lax.rem(hz + step, m)).start()

    total = own_share
    for step in range(1, m):
        other = lax.rem(hz + step, m)
        pltpu.make_async_remote_copy(
            src_ref=part.at[other], dst_ref=got.at[other],
            send_sem=pg_send.at[other], recv_sem=pg_recv.at[other],
            device_id=(me, other), device_id_type=MESH,
        ).wait_recv()
        total = total + got[other].astype(jnp.float32)
    qd[me] = jnp.concatenate([q_ref[...], total.astype(jnp.bfloat16)], axis=0).T

    @pl.when(parity == 1)
    def _():
        seq_copy(qd, qd_send, qd_recv, me, sibling).start()

    def send_qd(i, carry):
        seq_copy(qd, qd_send, qd_recv, me, 2 * (pair - 1 - i) + parity).start()
        return carry

    lax.fori_loop(0, pair, send_qd, 0)
    own_g = qd[me][:, high]
    for h in range(heads):
        dom[h] = jnp.where(high_mask(h), own_g, zero_16)

    product = attended * own_g.astype(jnp.float32)
    stat_lane = lax.broadcasted_iota(jnp.int32, (rows, 128), 1)
    stats = jnp.zeros((rows, 128), jnp.float32)
    for h in range(heads):
        row_dot = jnp.sum(jnp.where(high_mask(h), product, 0.0), axis=1, keepdims=True)
        log_total = max_s[h] + jnp.log2(sum_s[h])
        max_s[h] = log_total
        dot_s[h] = row_dot
        stats = jnp.where(stat_lane == h, log_total, stats)
        stats = jnp.where(stat_lane == heads + h, row_dot, stats)
    lr[me] = stats.T[:stat_rows, :]

    def send_lr(j, carry):
        seq_copy(lr, lr_send, lr_recv, me, j).start()
        return carry

    lax.fori_loop(0, me, send_lr, 0)

    def query_step(block, h, own):
        s = nt(qm[h], block[:, low]) * factor
        if own:
            s = jnp.where(col_id <= row_id, s, masked_score)
        p = jnp.exp2(s - max_s[h])
        ds = p * (nt(dom[h], block[:, high]) - dot_s[h])
        return nn(ds.astype(jnp.bfloat16), block[:, low])

    for h in range(heads):
        acc_a[h] = query_step(kv.at[me], h, True)

    def query_loop(i, carry):
        block = kv.at[i]
        for h in range(heads):
            acc_a[h] = acc_a[h] + query_step(block, h, False)
        return carry

    lax.fori_loop(0, me, query_loop, 0)
    query_sum = jnp.zeros((rows, wide), jnp.float32)
    for h in range(heads):
        query_sum = jnp.where(low_mask(h), acc_a[h], query_sum)
    qg_ref[...] = (query_sum * scale).T[:width, :].astype(jnp.bfloat16)

    def key_step(block, stat, h, own):
        s = nt(km[h], block[:, low]) * factor
        if own:
            s = jnp.where(row_id <= col_id, s, masked_score)
        p = jnp.exp2(s - stat[h:h + 1, :])
        value_part = nn(p.astype(jnp.bfloat16), block[:, high])
        ds = p * (nt(vm[h], block[:, high]) - stat[heads + h:heads + h + 1, :])
        return nn(ds.astype(jnp.bfloat16), block[:, low]), value_part

    for h in range(heads):
        acc_b[h], acc_c[h] = key_step(qd.at[me], lr.at[me], h, True)

    wpad[:, 0:pad, :] = jnp.zeros((m, pad, cols), jnp.bfloat16)
    wpad[:, pad + width:, :] = jnp.zeros((m, pad, cols), jnp.bfloat16)

    def project(slot):
        block = att.at[slot]
        return (
            nn(block[:, low], wpad[slot, pad:, :]),
            nn(block[:, high], wpad[slot, :wide, :]),
        )

    proj_top, proj_low = project(hz)
    for step in range(1, m):
        other = lax.rem(hz + step, m)
        att_copy(other, hz).wait_recv()
        more_top, more_low = project(other)
        proj_top = proj_top + more_top
        proj_low = proj_low + more_low
    proj_ref[:half, :] = proj_top.astype(jnp.bfloat16)
    proj_ref[half:, :] = proj_low.astype(jnp.bfloat16)

    def key_loop(i, carry):
        turn = i - (1 - parity) + 2
        same = (turn >= 2) & (lax.rem(turn, 2) == 0)
        j = 2 * (pair + lax.div(turn, 2)) + jnp.where(lax.rem(turn, 2) == 0, parity, 1 - parity)
        seq_copy(qd, qd_send, qd_recv, j, me).wait_recv()

        @pl.when(same)
        def _():
            pass_on(qd, qd_pass, qd_recv, j).start()

        seq_copy(lr, lr_send, lr_recv, j, me).wait_recv()
        for h in range(heads):
            key_part, value_part = key_step(qd.at[j], lr.at[j], h, False)
            acc_b[h] = acc_b[h] + key_part
            acc_c[h] = acc_c[h] + value_part
        return carry

    lax.fori_loop(0, n - 1 - me, key_loop, 0)
    key_sum = jnp.zeros((rows, wide), jnp.float32)
    value_sum = jnp.zeros((rows, wide), jnp.float32)
    for h in range(heads):
        key_sum = jnp.where(low_mask(h), acc_b[h], key_sum)
        value_sum = jnp.where(high_mask(h), acc_c[h], value_sum)
    kg_ref[...] = (key_sum * scale).T[:width, :].astype(jnp.bfloat16)
    vg_ref[...] = value_sum.T[pad:, :].astype(jnp.bfloat16)

    @pl.when(parity == 0)
    def _():
        seq_copy(kv, kv_send, kv_recv, me, sibling).wait_send()

    @pl.when(parity == 1)
    def _():
        seq_copy(qd, qd_send, qd_recv, me, sibling).wait_send()

    def sent_later(i, carry):
        seq_copy(kv, kv_send, kv_recv, me, 2 * i + parity).wait_send()
        pass_on(qd, qd_pass, qd_recv, 2 * i + parity).wait_send()
        return carry

    lax.fori_loop(pair + 1, n // 2, sent_later, 0)

    def sent_earlier(i, carry):
        seq_copy(qd, qd_send, qd_recv, me, 2 * i + parity).wait_send()
        pass_on(kv, kv_pass, kv_recv, 2 * i + parity).wait_send()
        return carry

    lax.fori_loop(0, pair, sent_earlier, 0)

    def sent_lr(j, carry):
        seq_copy(lr, lr_send, lr_recv, me, j).wait_send()
        return carry

    lax.fori_loop(0, me, sent_lr, 0)
    for step in range(1, m):
        other = lax.rem(hz + step, m)
        part_copy(other).wait_send()
        att_copy(hz, other).wait_send()


def finish(*refs):
    count = len(refs) // 2
    for source, target in zip(refs[:count], refs[count:]):
        target[...] = source[...]


def per_device(n, m, queries, keys, values, out_weight, out_grad):
    rows, width = queries.shape
    cols = out_grad.shape[1]
    heads = width // HD
    wide = round_up(width, 128)
    pad = wide - width
    stat_rows = round_up(2 * heads, 8)
    bf16, f32 = jnp.bfloat16, jnp.float32
    in_vmem = pl.BlockSpec(memory_space=pltpu.VMEM)
    dma = pltpu.SemaphoreType.DMA
    macs = rows * rows * n * 9 * width + 2 * rows * width * m * cols
    shapes = (
        jax.ShapeDtypeStruct((rows, cols), bf16),
        jax.ShapeDtypeStruct((width, rows), bf16),
        jax.ShapeDtypeStruct((width, rows), bf16),
        jax.ShapeDtypeStruct((width, rows), bf16),
    )
    results = pl.pallas_call(
        functools.partial(kernel, n, m),
        out_shape=shapes,
        in_specs=[in_vmem, in_vmem, in_vmem, pl.BlockSpec(memory_space=pl.ANY), in_vmem],
        out_specs=(in_vmem,) * 4,
        scratch_shapes=[
            pltpu.VMEM((n, rows, 2 * width), bf16),
            pltpu.VMEM((n, rows, 2 * width), bf16),
            pltpu.VMEM((n, stat_rows, rows), f32),
            pltpu.VMEM((m, width, rows), bf16),
            pltpu.VMEM((m, width, rows), bf16),
            pltpu.VMEM((m, rows // 2, 2 * width), bf16),
            pltpu.VMEM((m, pad + width + pad, cols), bf16),
        ]
        + [pltpu.VMEM((heads, rows, wide), bf16)] * 4
        + [pltpu.VMEM((heads, rows, wide), f32)] * 3
        + [pltpu.VMEM((heads, rows, 1), f32)] * 3
        + [dma((m,))]
        + [dma((n,))] * 6
        + [dma((m,))] * 4
        + [dma((n,))] * 2,
        compiler_params=pltpu.CompilerParams(
            collective_id=0, has_side_effects=True, vmem_limit_bytes=56 * 1024 * 1024
        ),
        cost_estimate=pl.CostEstimate(
            flops=macs, bytes_accessed=6 * rows * width * 2, transcendentals=rows * rows * n * heads
        ),
    )(queries.T, keys.T, values.T, out_weight, out_grad)
    projected, query_grad, key_grad, value_grad = pl.pallas_call(
        finish, out_shape=shapes, in_specs=[in_vmem] * 4, out_specs=(in_vmem,) * 4
    )(*results)
    return projected, query_grad.T, key_grad.T, value_grad.T


def solution(mesh):
    return jax.shard_map(
        functools.partial(per_device, mesh.shape["seq"], mesh.shape["head"]),
        mesh=mesh,
        in_specs=(P("seq", "head"), P("seq", "head"), P("seq", "head"), P(), P("seq", "head")),
        out_specs=(P("seq", "head"), P("seq", "head"), P("seq", "head"), P("seq", "head")),
        check_vma=False,
    )
```

```python
import functools
import math

import jax
import jax.numpy as jnp
from jax import lax
from jax.experimental import pallas as pl
from jax.experimental.pallas import tpu as pltpu
from jax.sharding import PartitionSpec as P

HD = 64
MESH = pl.DeviceIdType.MESH
masked_score = -1e30


def round_up(value, unit):
    return -(-value // unit) * unit


def nt(left, right):
    return lax.dot_general(
        left, right, (((1,), (1,)), ((), ())), preferred_element_type=jnp.float32
    )


def nn(left, right):
    return jnp.dot(left, right, preferred_element_type=jnp.float32)


def kernel(
    n, m, q_ref, k_ref, v_ref, w_ref, og_ref,
    proj_ref, qg_ref, kg_ref, vg_ref,
    kv, qd, lr, part, got, att, wpad, qm, dom, km, vm,
    acc_a, acc_b, acc_c, max_s, dot_s, acc_t, max_r, sum_r,
    w_sem, kv_send, kv_recv, qd_send, qd_recv, lr_send, lr_recv,
    pg_send, pg_recv, at_send, at_recv, kv_pass, qd_pass,
):
    width, rows = q_ref.shape
    cols = og_ref.shape[1]
    heads = width // HD
    wide = round_up(width, 128)
    pad = wide - width
    low = slice(0, wide)
    high = slice(2 * width - wide, 2 * width)
    half = rows // 2
    stat_rows = lr.shape[1]
    scale = HD ** (-0.5)
    factor = scale / math.log(2.0)
    me = lax.axis_index("seq")
    hz = lax.axis_index("head")
    parity = lax.rem(me, 2)
    pair = lax.div(me, 2)
    sibling = 2 * pair + 1 - parity

    def w_copy(j):
        return pltpu.make_async_copy(
            w_ref.at[pl.ds(j * width, width), pl.ds(pl.multiple_of(hz * cols, 128), cols)],
            wpad.at[j, pl.ds(pad, width), :],
            w_sem.at[j],
        )

    for j in range(m):
        w_copy(j).start()

    barrier = pltpu.get_barrier_semaphore()
    for step in range(1, m):
        other = lax.rem(hz + step, m)
        pl.semaphore_signal(barrier, inc=1, device_id=(me, other), device_id_type=MESH)

    def greet(step, carry):
        other = lax.rem(me + step, n)
        pl.semaphore_signal(barrier, inc=1, device_id=(other, hz), device_id_type=MESH)
        return carry

    lax.fori_loop(1, n, greet, 0)

    kv[me] = jnp.concatenate([k_ref[...], v_ref[...]], axis=0).T
    pl.semaphore_wait(barrier, n - 1 + m - 1)

    def seq_copy(buf, send, recv, slot, dst):
        return pltpu.make_async_remote_copy(
            src_ref=buf.at[slot], dst_ref=buf.at[slot],
            send_sem=send.at[dst], recv_sem=recv.at[slot],
            device_id=(dst, hz), device_id_type=MESH,
        )

    def pass_on(buf, send, recv, slot):
        return pltpu.make_async_remote_copy(
            src_ref=buf.at[slot], dst_ref=buf.at[slot],
            send_sem=send.at[slot], recv_sem=recv.at[slot],
            device_id=(sibling, hz), device_id_type=MESH,
        )

    @pl.when(parity == 0)
    def _():
        seq_copy(kv, kv_send, kv_recv, me, sibling).start()

    def send_kv(i, carry):
        seq_copy(kv, kv_send, kv_recv, me, 2 * i + parity).start()
        return carry

    lax.fori_loop(pair + 1, n // 2, send_kv, 0)

    for j in range(m):
        w_copy(j).wait()

    def share(j):
        return nt(wpad[j, pad:pad + width, :], og_ref[...])

    def part_copy(dst):
        return pltpu.make_async_remote_copy(
            src_ref=part.at[dst], dst_ref=got.at[hz],
            send_sem=pg_send.at[dst], recv_sem=pg_recv.at[hz],
            device_id=(me, dst), device_id_type=MESH,
        )

    for step in range(1, m):
        other = lax.rem(hz + step, m)
        part[other] = share(other).astype(jnp.bfloat16)
        part_copy(other).start()
    own_share = share(hz)

    lane = lax.broadcasted_iota(jnp.int32, (rows, wide), 1)

    def low_mask(h):
        return (lane >= h * HD) & (lane < (h + 1) * HD)

    def high_mask(h):
        return (lane >= pad + h * HD) & (lane < pad + (h + 1) * HD)

    q_wide = jnp.concatenate([q_ref[...], jnp.zeros((pad, rows), jnp.bfloat16)], axis=0).T
    zero_16 = jnp.zeros((rows, wide), jnp.bfloat16)
    own_k = kv[me][:, low]
    own_v = kv[me][:, high]
    for h in range(heads):
        qm[h] = jnp.where(low_mask(h), q_wide, zero_16)
        km[h] = jnp.where(low_mask(h), own_k, zero_16)
        vm[h] = jnp.where(high_mask(h), own_v, zero_16)

    row_id = lax.broadcasted_iota(jnp.int32, (rows, rows), 0)
    col_id = lax.broadcasted_iota(jnp.int32, (rows, rows), 1)

    for h in range(heads):
        s = nt(own_k, qm[h]) * factor
        s = jnp.where(row_id <= col_id, s, masked_score)
        top = jnp.max(s, axis=0, keepdims=True)
        e = jnp.exp2(s - top)
        max_r[h] = top
        sum_r[h] = jnp.sum(e, axis=0, keepdims=True)
        acc_t[h] = nn(v_ref[h * HD:(h + 1) * HD, :], e.astype(jnp.bfloat16))

    def forward(i, carry):
        turn = i - parity + 2
        same = (turn >= 2) & (lax.rem(turn, 2) == 0)
        j = 2 * (pair - lax.div(turn, 2)) + jnp.where(lax.rem(turn, 2) == 0, parity, 1 - parity)
        seq_copy(kv, kv_send, kv_recv, j, me).wait_recv()

        @pl.when(same)
        def _():
            pass_on(kv, kv_pass, kv_recv, j).start()

        block = kv.at[j]
        value_t = block[:, high].T
        for h in range(heads):
            s = nt(block[:, low], qm[h]) * factor
            old = max_r[h]
            top = jnp.maximum(old, jnp.max(s, axis=0, keepdims=True))
            alpha = jnp.exp2(old - top)
            e = jnp.exp2(s - top)
            max_r[h] = top
            sum_r[h] = sum_r[h] * alpha + jnp.sum(e, axis=0, keepdims=True)
            value_h = value_t[pad + h * HD:pad + (h + 1) * HD, :]
            acc_t[h] = acc_t[h] * alpha + nn(value_h, e.astype(jnp.bfloat16))
        return carry

    lax.fori_loop(0, me, forward, 0)

    mixed = [jnp.zeros((pad, rows), jnp.float32)]
    for h in range(heads):
        mixed.append(acc_t[h] * (1.0 / sum_r[h]))
    attended_t = jnp.concatenate(mixed, axis=0).astype(jnp.bfloat16).astype(jnp.float32)
    attended = attended_t.T
    upper = attended[:half, pad:]
    lower = attended[half:, pad:]
    att[hz] = jnp.concatenate([upper, lower], axis=1).astype(jnp.bfloat16)

    def att_copy(slot, dst):
        return pltpu.make_async_remote_copy(
            src_ref=att.at[slot], dst_ref=att.at[slot],
            send_sem=at_send.at[dst], recv_sem=at_recv.at[slot],
            device_id=(me, dst), device_id_type=MESH,
        )

    for step in range(1, m):
        att_copy(hz, lax.rem(hz + step, m)).start()

    total = own_share
    for step in range(1, m):
        other = lax.rem(hz + step, m)
        pltpu.make_async_remote_copy(
            src_ref=part.at[other], dst_ref=got.at[other],
            send_sem=pg_send.at[other], recv_sem=pg_recv.at[other],
            device_id=(me, other), device_id_type=MESH,
        ).wait_recv()
        total = total + got[other].astype(jnp.float32)
    qd[me] = jnp.concatenate([q_ref[...], total.astype(jnp.bfloat16)], axis=0).T

    @pl.when(parity == 1)
    def _():
        seq_copy(qd, qd_send, qd_recv, me, sibling).start()

    def send_qd(i, carry):
        seq_copy(qd, qd_send, qd_recv, me, 2 * (pair - 1 - i) + parity).start()
        return carry

    lax.fori_loop(0, pair, send_qd, 0)
    own_g = qd[me][:, high]
    for h in range(heads):
        dom[h] = jnp.where(high_mask(h), own_g, zero_16)

    product = attended_t[pad:, :] * total.astype(jnp.bfloat16).astype(jnp.float32)
    stat_row = lax.broadcasted_iota(jnp.int32, (128, rows), 0)
    stats = jnp.zeros((128, rows), jnp.float32)
    for h in range(heads):
        row_dot = jnp.sum(product[h * HD:(h + 1) * HD, :], axis=0, keepdims=True)
        stats = jnp.where(stat_row == h, max_r[h] + jnp.log2(sum_r[h]), stats)
        stats = jnp.where(stat_row == heads + h, row_dot, stats)
    lr[me] = stats[:stat_rows, :]
    columns = stats.T
    for h in range(heads):
        max_s[h] = columns[:, h:h + 1]
        dot_s[h] = columns[:, heads + h:heads + h + 1]

    def send_lr(j, carry):
        seq_copy(lr, lr_send, lr_recv, me, j).start()
        return carry

    lax.fori_loop(0, me, send_lr, 0)

    def query_step(block, h, own):
        s = nt(qm[h], block[:, low]) * factor
        if own:
            s = jnp.where(col_id <= row_id, s, masked_score)
        p = jnp.exp2(s - max_s[h])
        ds = p * (nt(dom[h], block[:, high]) - dot_s[h])
        return nn(ds.astype(jnp.bfloat16), block[:, low])

    for h in range(heads):
        acc_a[h] = query_step(kv.at[me], h, True)

    def query_loop(i, carry):
        block = kv.at[i]
        for h in range(heads):
            acc_a[h] = acc_a[h] + query_step(block, h, False)
        return carry

    lax.fori_loop(0, me, query_loop, 0)
    query_sum = jnp.zeros((rows, wide), jnp.float32)
    for h in range(heads):
        query_sum = jnp.where(low_mask(h), acc_a[h], query_sum)
    qg_ref[...] = (query_sum * scale).T[:width, :].astype(jnp.bfloat16)

    def key_step(block, stat, h, own):
        s = nt(km[h], block[:, low]) * factor
        if own:
            s = jnp.where(row_id <= col_id, s, masked_score)
        p = jnp.exp2(s - stat[h:h + 1, :])
        value_part = nn(p.astype(jnp.bfloat16), block[:, high])
        ds = p * (nt(vm[h], block[:, high]) - stat[heads + h:heads + h + 1, :])
        return nn(ds.astype(jnp.bfloat16), block[:, low]), value_part

    for h in range(heads):
        acc_b[h], acc_c[h] = key_step(qd.at[me], lr.at[me], h, True)

    wpad[:, 0:pad, :] = jnp.zeros((m, pad, cols), jnp.bfloat16)
    wpad[:, pad + width:, :] = jnp.zeros((m, pad, cols), jnp.bfloat16)

    def project(slot):
        block = att.at[slot]
        return (
            nn(block[:, low], wpad[slot, pad:, :]),
            nn(block[:, high], wpad[slot, :wide, :]),
        )

    proj_top, proj_low = project(hz)
    for step in range(1, m):
        other = lax.rem(hz + step, m)
        att_copy(other, hz).wait_recv()
        more_top, more_low = project(other)
        proj_top = proj_top + more_top
        proj_low = proj_low + more_low
    proj_ref[:half, :] = proj_top.astype(jnp.bfloat16)
    proj_ref[half:, :] = proj_low.astype(jnp.bfloat16)

    def key_loop(i, carry):
        turn = i - (1 - parity) + 2
        same = (turn >= 2) & (lax.rem(turn, 2) == 0)
        j = 2 * (pair + lax.div(turn, 2)) + jnp.where(lax.rem(turn, 2) == 0, parity, 1 - parity)
        seq_copy(qd, qd_send, qd_recv, j, me).wait_recv()

        @pl.when(same)
        def _():
            pass_on(qd, qd_pass, qd_recv, j).start()

        seq_copy(lr, lr_send, lr_recv, j, me).wait_recv()
        for h in range(heads):
            key_part, value_part = key_step(qd.at[j], lr.at[j], h, False)
            acc_b[h] = acc_b[h] + key_part
            acc_c[h] = acc_c[h] + value_part
        return carry

    lax.fori_loop(0, n - 1 - me, key_loop, 0)
    key_sum = jnp.zeros((rows, wide), jnp.float32)
    value_sum = jnp.zeros((rows, wide), jnp.float32)
    for h in range(heads):
        key_sum = jnp.where(low_mask(h), acc_b[h], key_sum)
        value_sum = jnp.where(high_mask(h), acc_c[h], value_sum)
    kg_ref[...] = (key_sum * scale).T[:width, :].astype(jnp.bfloat16)
    vg_ref[...] = value_sum.T[pad:, :].astype(jnp.bfloat16)

    @pl.when(parity == 0)
    def _():
        seq_copy(kv, kv_send, kv_recv, me, sibling).wait_send()

    @pl.when(parity == 1)
    def _():
        seq_copy(qd, qd_send, qd_recv, me, sibling).wait_send()

    def sent_later(i, carry):
        seq_copy(kv, kv_send, kv_recv, me, 2 * i + parity).wait_send()
        pass_on(qd, qd_pass, qd_recv, 2 * i + parity).wait_send()
        return carry

    lax.fori_loop(pair + 1, n // 2, sent_later, 0)

    def sent_earlier(i, carry):
        seq_copy(qd, qd_send, qd_recv, me, 2 * i + parity).wait_send()
        pass_on(kv, kv_pass, kv_recv, 2 * i + parity).wait_send()
        return carry

    lax.fori_loop(0, pair, sent_earlier, 0)

    def sent_lr(j, carry):
        seq_copy(lr, lr_send, lr_recv, me, j).wait_send()
        return carry

    lax.fori_loop(0, me, sent_lr, 0)
    for step in range(1, m):
        other = lax.rem(hz + step, m)
        part_copy(other).wait_send()
        att_copy(hz, other).wait_send()


def finish(*refs):
    count = len(refs) // 2
    for source, target in zip(refs[:count], refs[count:]):
        target[...] = source[...]


def per_device(n, m, queries, keys, values, out_weight, out_grad):
    rows, width = queries.shape
    cols = out_grad.shape[1]
    heads = width // HD
    wide = round_up(width, 128)
    pad = wide - width
    stat_rows = round_up(2 * heads, 8)
    bf16, f32 = jnp.bfloat16, jnp.float32
    in_vmem = pl.BlockSpec(memory_space=pltpu.VMEM)
    dma = pltpu.SemaphoreType.DMA
    macs = rows * rows * n * 9 * width + 2 * rows * width * m * cols
    shapes = (
        jax.ShapeDtypeStruct((rows, cols), bf16),
        jax.ShapeDtypeStruct((width, rows), bf16),
        jax.ShapeDtypeStruct((width, rows), bf16),
        jax.ShapeDtypeStruct((width, rows), bf16),
    )
    results = pl.pallas_call(
        functools.partial(kernel, n, m),
        out_shape=shapes,
        in_specs=[in_vmem, in_vmem, in_vmem, pl.BlockSpec(memory_space=pl.ANY), in_vmem],
        out_specs=(in_vmem,) * 4,
        scratch_shapes=[
            pltpu.VMEM((n, rows, 2 * width), bf16),
            pltpu.VMEM((n, rows, 2 * width), bf16),
            pltpu.VMEM((n, stat_rows, rows), f32),
            pltpu.VMEM((m, width, rows), bf16),
            pltpu.VMEM((m, width, rows), bf16),
            pltpu.VMEM((m, rows // 2, 2 * width), bf16),
            pltpu.VMEM((m, pad + width + pad, cols), bf16),
        ]
        + [pltpu.VMEM((heads, rows, wide), bf16)] * 4
        + [pltpu.VMEM((heads, rows, wide), f32)] * 3
        + [pltpu.VMEM((heads, rows, 1), f32)] * 2
        + [pltpu.VMEM((heads, HD, rows), f32)]
        + [pltpu.VMEM((heads, 1, rows), f32)] * 2
        + [dma((m,))]
        + [dma((n,))] * 6
        + [dma((m,))] * 4
        + [dma((n,))] * 2,
        compiler_params=pltpu.CompilerParams(
            collective_id=0, has_side_effects=True, vmem_limit_bytes=56 * 1024 * 1024
        ),
        cost_estimate=pl.CostEstimate(
            flops=macs, bytes_accessed=6 * rows * width * 2, transcendentals=rows * rows * n * heads
        ),
    )(queries.T, keys.T, values.T, out_weight, out_grad)
    projected, query_grad, key_grad, value_grad = pl.pallas_call(
        finish, out_shape=shapes, in_specs=[in_vmem] * 4, out_specs=(in_vmem,) * 4
    )(*results)
    return projected, query_grad.T, key_grad.T, value_grad.T


def solution(mesh):
    return jax.shard_map(
        functools.partial(per_device, mesh.shape["seq"], mesh.shape["head"]),
        mesh=mesh,
        in_specs=(P("seq", "head"), P("seq", "head"), P("seq", "head"), P(), P("seq", "head")),
        out_specs=(P("seq", "head"), P("seq", "head"), P("seq", "head"), P("seq", "head")),
        check_vma=False,
    )
```
